32 devices in a mesh: grp: 2 (over y), az: 4 (over z), sec: 2 (over core), sub: 2 (over x).
Axes of the slice: x: 2, y: 2, z: 4, core: 2. Of those that a mesh axis runs over, the one named last changes fastest.
Arguments:
- echoes: bfloat16 [2, 4096, 32768], P(None, ('grp', 'az', 'sec'), 'sub'), parts along dimension 1, may hold values from -6 to 6
- chirp_taps: float32 [2, 2048], replicated, may hold values from -0.09375 to 0.09375
- replicas: bfloat16 [2, 1024, 65536], P(None, None, ('grp', 'az', 'sec', 'sub')), parts along dimension 2, may hold values from -0.125 to 0.125
- lengths: int32 [65536], P(('grp', 'az', 'sec', 'sub')), parts along dimension 0, may hold values from 128 to 1024, as said below
Outputs:
- focused: bfloat16 [2, 2048, 65536], P(None, None, ('grp', 'az', 'sec', 'sub')), parts along dimension 2
The draws below stay inside these ranges and needn't reach their ends.
There are 2 independent parts, one for each index of `grp`. The reference program is written for one: setup_inputs(seed, part) draws one part's arguments, and reference() takes and returns one part's arrays. A program takes and returns all parts, laid end to end along the dimension named above; an argument that names none is the same for every part. Nothing has to cross between parts.
Inputs may be any that keep to these rules, and one draw needn't show every extreme that they name: `lengths`: count of the leading taps of each range bin's azimuth replica that belong to it.
All inputs are finite; a program needn't handle non-finite values.
Results may differ from the reference program's by a relative error of at most 0.013.
Values may be sent and summed in bfloat16 or wider, within the bound.
A program may use at most 320 MiB of HBM per device.

```python
import math
import jax
import jax.numpy as jnp
from jax import lax

R1 = 256
R2 = 128
A1 = 32
A2 = 64
CHIRP = 2048
TAPS = 1024
RANGE = 32768
PULSES = 2048


def draw_lengths(key, part):
    shortest = TAPS // 8
    base_len = jax.random.randint(key, (RANGE,), shortest, TAPS + 1, dtype=jnp.int32)
    top_at = jax.random.randint(jax.random.fold_in(key, 1), (), 0, RANGE, dtype=jnp.int32)
    step_away = jax.random.randint(jax.random.fold_in(key, 2), (), 0, RANGE - 1, dtype=jnp.int32)
    low_at = (top_at + 1 + step_away) % RANGE
    base_len = base_len.at[top_at].set(TAPS)
    return base_len.at[low_at].set(shortest)


def levels(key, extent, split, least, high):
    factor_of = 1.0
    for position, blocks in split:
        heights = jax.random.uniform(jax.random.fold_in(jax.random.fold_in(key, 6), position), (blocks,), jnp.float32, least / len(split), high / len(split))
        factor_of = factor_of * jnp.repeat(jnp.exp(heights), extent[position] // blocks).reshape((-1,) + (1,) * (len(extent) - 1 - position))
    return factor_of


def bell_draw(stream_key, extent, deviation, limit, cuts=(), kind=jnp.bfloat16):
    gain = levels(stream_key, extent, cuts, -0.22, 0.18) if cuts else 1.0
    values = jax.random.normal(stream_key, extent, jnp.float32) * deviation * gain
    return jnp.minimum(jnp.maximum(values, -limit), limit).astype(kind)


def setup_inputs(seed: int = 0, part: int = 0) -> dict:
    key_of = jax.random.split(jax.random.key(seed), 5)
    part_splits = jax.random.split(jax.random.fold_in(key_of[4], part), 5)
    echoes = bell_draw(part_splits[0], (2, PULSES, RANGE), 1.0, 6.0, ((1, 8), (2, 2)))
    chirp_taps = bell_draw(key_of[1], (2, CHIRP), (2 * CHIRP) ** -0.5, 0.09375, (), jnp.float32)
    replicas = bell_draw(part_splits[2], (2, TAPS, RANGE), (2 * TAPS) ** -0.5, 0.125, ((2, 16),))
    lengths = draw_lengths(jax.random.fold_in(jax.random.fold_in(key_of[4], part), 71), part)
    return dict(echoes=echoes, chirp_taps=chirp_taps, replicas=replicas, lengths=lengths)


HIGHEST_PRECISION = lax.Precision.HIGHEST


def dft_table(length, direction, value_type):
    positions = jnp.arange(length, dtype=jnp.int32)
    phases = (positions[:, None] * positions[None, :]) % length
    angles = (direction * 2.0 * math.pi / length) * phases.astype(jnp.float32)
    return jnp.cos(angles).astype(value_type), jnp.sin(angles).astype(value_type)


def twiddles(rows_count, cols_count, length, direction):
    first_side = jnp.arange(rows_count, dtype=jnp.int32)
    second = jnp.arange(cols_count, dtype=jnp.int32)
    phases = (first_side[:, None] * second[None, :]) % length
    angles = (direction * 2.0 * math.pi / length) * phases.astype(jnp.float32)
    return jnp.cos(angles), jnp.sin(angles)


def contract(pattern, left_real, left_imag, right_real, right_imag):
    def single(left_side, right_side):
        return jnp.einsum(pattern, left_side.astype(jnp.float32), right_side.astype(jnp.float32), precision=HIGHEST_PRECISION)
    return (single(left_real, right_real) - single(left_imag, right_imag),
            single(left_real, right_imag) + single(left_imag, right_real))


def product(first_real, first_imag, second_real, second_imag):
    return (first_real * second_real - first_imag * second_imag,
            first_real * second_imag + first_imag * second_real)


def chirp_spectrum(taps_real, taps_imag, lead_rows):
    padded_real = jnp.pad(taps_real, (0, lead_rows * R2 - CHIRP)).reshape(lead_rows, R2)
    padded_imag = jnp.pad(taps_imag, (0, lead_rows * R2 - CHIRP)).reshape(lead_rows, R2)
    table_real, table_imag = dft_table(R1, -1.0, jnp.float32)
    step_real, step_imag = contract("ab,ak->kb", padded_real, padded_imag, table_real[:lead_rows], table_imag[:lead_rows])
    turn_real, turn_imag = twiddles(R1, R2, RANGE, -1.0)
    step_real, step_imag = product(step_real, step_imag, turn_real, turn_imag)
    second_real, second_imag = dft_table(R2, -1.0, jnp.float32)
    return contract("kb,bm->km", step_real, step_imag, second_real, second_imag)


def range_rows(real_rows, imag_rows, filter_real, filter_imag):
    row_count = real_rows.shape[0]
    grid_real = real_rows.reshape(row_count, R1, R2)
    grid_imag = imag_rows.reshape(row_count, R1, R2)
    fwd_first = dft_table(R1, -1.0, jnp.bfloat16)
    fwd_second = dft_table(R2, -1.0, jnp.bfloat16)
    inv_first = dft_table(R1, 1.0, jnp.bfloat16)
    inv_second = dft_table(R2, 1.0, jnp.bfloat16)
    turn_fwd = twiddles(R1, R2, RANGE, -1.0)
    turn_inv = twiddles(R1, R2, RANGE, 1.0)
    step_real, step_imag = contract("rab,ak->rkb", grid_real, grid_imag, fwd_first[0], fwd_first[1])
    step_real, step_imag = product(step_real, step_imag, turn_fwd[0], turn_fwd[1])
    step_real, step_imag = step_real.astype(jnp.bfloat16), step_imag.astype(jnp.bfloat16)
    spec_real, spec_imag = contract("rkb,bm->rkm", step_real, step_imag, fwd_second[0], fwd_second[1])
    spec_real, spec_imag = product(spec_real, spec_imag, filter_real, filter_imag)
    spec_real, spec_imag = spec_real.astype(jnp.bfloat16), spec_imag.astype(jnp.bfloat16)
    back_real, back_imag = contract("rkm,md->rkd", spec_real, spec_imag, inv_second[0], inv_second[1])
    back_real, back_imag = product(back_real, back_imag, turn_inv[0], turn_inv[1])
    back_real, back_imag = back_real.astype(jnp.bfloat16), back_imag.astype(jnp.bfloat16)
    out_real, out_imag = contract("rkd,kc->rcd", back_real, back_imag, inv_first[0], inv_first[1])
    return (out_real.astype(jnp.bfloat16).reshape(row_count, RANGE),
            out_imag.astype(jnp.bfloat16).reshape(row_count, RANGE))


def replica_spectrum(taps_real, taps_imag, counts, lead_rows):
    bin_count = taps_real.shape[1]
    kept_taps = jnp.arange(TAPS, dtype=jnp.int32)[:, None] < counts[None, :]
    taps_real = jnp.where(kept_taps, taps_real, jnp.zeros_like(taps_real))
    taps_imag = jnp.where(kept_taps, taps_imag, jnp.zeros_like(taps_imag))
    extra_rows = lead_rows * A2 - TAPS
    grid_real = jnp.pad(taps_real, ((0, extra_rows), (0, 0))).reshape(lead_rows, A2, bin_count)
    grid_imag = jnp.pad(taps_imag, ((0, extra_rows), (0, 0))).reshape(lead_rows, A2, bin_count)
    table_real, table_imag = dft_table(A1, -1.0, jnp.bfloat16)
    step_real, step_imag = contract("abn,ak->kbn", grid_real, grid_imag, table_real[:lead_rows], table_imag[:lead_rows])
    turn_real, turn_imag = twiddles(A1, A2, PULSES, -1.0)
    step_real, step_imag = product(step_real, step_imag, turn_real[:, :, None], turn_imag[:, :, None])
    step_real, step_imag = step_real.astype(jnp.bfloat16), step_imag.astype(jnp.bfloat16)
    second_real, second_imag = dft_table(A2, -1.0, jnp.bfloat16)
    return contract("kbn,bm->kmn", step_real, step_imag, second_real, second_imag)


def focus_bins(column_real, column_imag, spec_real, spec_imag):
    bin_count = column_real.shape[1]
    grid_real = column_real.reshape(A1, A2, bin_count)
    grid_imag = column_imag.reshape(A1, A2, bin_count)
    fwd_first = dft_table(A1, -1.0, jnp.bfloat16)
    fwd_second = dft_table(A2, -1.0, jnp.bfloat16)
    inv_first = dft_table(A1, 1.0, jnp.bfloat16)
    inv_second = dft_table(A2, 1.0, jnp.bfloat16)
    turn_fwd = twiddles(A1, A2, PULSES, -1.0)
    turn_inv = twiddles(A1, A2, PULSES, 1.0)
    step_real, step_imag = contract("abn,ak->kbn", grid_real, grid_imag, fwd_first[0], fwd_first[1])
    step_real, step_imag = product(step_real, step_imag, turn_fwd[0][:, :, None], turn_fwd[1][:, :, None])
    step_real, step_imag = step_real.astype(jnp.bfloat16), step_imag.astype(jnp.bfloat16)
    freq_real, freq_imag = contract("kbn,bm->kmn", step_real, step_imag, fwd_second[0], fwd_second[1])
    freq_real, freq_imag = product(freq_real, freq_imag, spec_real, -spec_imag)
    scale_factor = 1.0 / PULSES
    freq_real = (freq_real * scale_factor).astype(jnp.bfloat16)
    freq_imag = (freq_imag * scale_factor).astype(jnp.bfloat16)
    back_real, back_imag = contract("kmn,md->kdn", freq_real, freq_imag, inv_second[0], inv_second[1])
    back_real, back_imag = product(back_real, back_imag, turn_inv[0][:, :, None], turn_inv[1][:, :, None])
    back_real, back_imag = back_real.astype(jnp.bfloat16), back_imag.astype(jnp.bfloat16)
    out_real, out_imag = contract("kdn,kc->cdn", back_real, back_imag, inv_first[0], inv_first[1])
    return (out_real.astype(jnp.bfloat16).reshape(PULSES, bin_count),
            out_imag.astype(jnp.bfloat16).reshape(PULSES, bin_count))


def reference(echoes, chirp_taps, replicas, lengths):
    spec_real, spec_imag = chirp_spectrum(chirp_taps[0], chirp_taps[1], R1)
    filter_real = spec_real / RANGE
    filter_imag = -spec_imag / RANGE
    row_block = min(256, PULSES)
    grouped = echoes.reshape(2, PULSES // row_block, row_block, RANGE).transpose(1, 0, 2, 3)

    def compress(piece):
        out_real, out_imag = range_rows(piece[0], piece[1], filter_real, filter_imag)
        return jnp.stack([out_real, out_imag])

    compressed = lax.map(compress, grouped).transpose(1, 0, 2, 3).reshape(2, PULSES, RANGE)
    bin_block = min(512, RANGE)
    block_count = RANGE // bin_block
    columns_all = compressed.reshape(2, PULSES, block_count, bin_block).transpose(2, 0, 1, 3)
    replica_all = replicas.reshape(2, TAPS, block_count, bin_block).transpose(2, 0, 1, 3)
    count_rows = lengths.reshape(block_count, bin_block)

    def focus(pieces):
        column, replica, count_row = pieces
        replica_real, replica_imag = replica_spectrum(replica[0], replica[1], count_row, A1)
        result_real, result_imag = focus_bins(column[0], column[1], replica_real, replica_imag)
        return jnp.stack([result_real, result_imag])

    result = lax.map(focus, (columns_all, replica_all, count_rows))
    return result.transpose(1, 2, 0, 3).reshape(2, PULSES, RANGE)
```

```python
import functools
import math

import jax
import jax.numpy as jnp
import numpy as np
from jax import lax
from jax.experimental import pallas as pl
from jax.experimental.pallas import tpu as pltpu
from jax.sharding import PartitionSpec as P

CHIRP = 2048
TAPS = 1024
PULSES = 2048
QUARTER = PULSES // 4
CHUNKS = 2


def azimuth_tables():
    j = np.arange(QUARTER)[:, None]
    b = np.arange(QUARTER)[None, :]
    tables = []
    for t in range(4):
        angles = -2.0 * math.pi / PULSES * ((b * (4 * j + t)) % PULSES)
        cosine, sine = np.cos(angles), np.sin(angles)
        tables.append(np.block([[cosine, -sine], [sine, cosine]]))
    return np.stack(tables).astype(np.float32).astype(jnp.bfloat16)


def toeplitz(taps, width):
    depth = CHIRP + width
    length = depth + width
    padded = jnp.pad(taps, (0, length - CHIRP))
    flat = jnp.tile(padded, width)[: width * (length - 1)]
    return flat.reshape(width, length - 1)[:, :depth].T


def range_kernel(width, order, echo_ref, real_ref, imag_ref, out_ref):
    start = pl.multiple_of(order(pl.program_id(0)) * width, width)
    depth = CHIRP + width
    both = jnp.dot(
        echo_ref[0, :, pl.ds(start, depth)], real_ref[...], preferred_element_type=jnp.float32
    ) + jnp.dot(
        echo_ref[1, :, pl.ds(start, depth)], imag_ref[...], preferred_element_type=jnp.float32
    )
    out_ref[0, 0, 0] = both[:, :width].astype(jnp.bfloat16)
    out_ref[0, 0, 1] = both[:, width:].astype(jnp.bfloat16)


def compress(
    extended, real_table, imag_table, chunk, chunks, sub_count, outer_count, own_bins
):
    rows = extended.shape[1]
    width = real_table.shape[1] // 2
    chunk_bins = own_bins // chunks
    per_chunk = chunk_bins // width
    per_dest = own_bins // width

    def order(step):
        return (step // per_chunk) * per_dest + chunk * per_chunk + step % per_chunk

    def place(step):
        dest = step // per_chunk
        return (dest % sub_count, dest // sub_count, 0, 0, step % per_chunk)

    whole = lambda *shape: pl.BlockSpec(
        shape, lambda step: (0,) * len(shape), pipeline_mode=pl.Buffered(1)
    )
    steps = outer_count * per_chunk
    return pl.pallas_call(
        functools.partial(range_kernel, width, order),
        grid=(steps,),
        in_specs=[
            whole(*extended.shape),
            whole(*real_table.shape),
            whole(*imag_table.shape),
        ],
        out_specs=pl.BlockSpec((1, 1, 2, rows, width), place),
        out_shape=jax.ShapeDtypeStruct(
            (sub_count, outer_count // sub_count, 2, rows, chunk_bins), jnp.bfloat16
        ),
        compiler_params=pltpu.CompilerParams(vmem_limit_bytes=48 * 1024 * 1024),
        cost_estimate=pl.CostEstimate(
            flops=steps * 4 * rows * real_table.shape[0] * 2 * width,
            bytes_accessed=2 * extended.size + 2 * steps * 2 * rows * width,
            transcendentals=0,
        ),
    )(extended, real_table, imag_table)


def turn(pair, count):
    real, imag = pair
    return ((real, imag), (-imag, real), (-real, -imag), (imag, -real))[count % 4]


def combine(pairs, direction, t):
    turned = [turn(pair, direction * a * t) for a, pair in enumerate(pairs)]
    real, imag = turned[0]
    for other_real, other_imag in turned[1:]:
        real, imag = real + other_real, imag + other_imag
    return real, imag


def azimuth_kernel(column_ref, replica_ref, count_ref, fwd_ref, inv_ref, out_ref):
    bins = out_ref.shape[-1]
    f32 = jnp.float32
    column = [column_ref[:, s].reshape(4, QUARTER, bins) for s in range(2)]
    column = [(column[0][a].astype(f32), column[1][a].astype(f32)) for a in range(4)]
    position = lax.broadcasted_iota(jnp.int32, (TAPS, bins), 0)
    kept = position < count_ref[...]
    taps = [jnp.where(kept, replica_ref[s].astype(f32), 0.0) for s in range(2)]
    taps = [
        (taps[0][a * QUARTER : (a + 1) * QUARTER], taps[1][a * QUARTER : (a + 1) * QUARTER])
        for a in range(TAPS // QUARTER)
    ]
    parts = []
    for t in range(4):
        sides = []
        for pieces in (column, taps):
            mixed = jnp.concatenate(combine(pieces, -1, t), axis=0).astype(jnp.bfloat16)
            found = jnp.dot(fwd_ref[t], mixed, preferred_element_type=f32)
            sides.append((found[:QUARTER], found[QUARTER:]))
        (x_real, x_imag), (q_real, q_imag) = sides
        y_real = (x_real * q_real + x_imag * q_imag) * (1.0 / PULSES)
        y_imag = (x_imag * q_real - x_real * q_imag) * (1.0 / PULSES)
        y = jnp.concatenate([y_real, y_imag], axis=0).astype(jnp.bfloat16)
        back = jnp.dot(inv_ref[t], y, preferred_element_type=f32)
        parts.append((back[:QUARTER], back[QUARTER:]))
    for a in range(4):
        real, imag = combine(parts, 1, a)
        out_ref[0, a * QUARTER : (a + 1) * QUARTER] = real.astype(jnp.bfloat16)
        out_ref[1, a * QUARTER : (a + 1) * QUARTER] = imag.astype(jnp.bfloat16)


def focus(columns, replicas, lengths, fwd, inv, chunk):
    outer_count, _, rows, chunk_bins = columns.shape
    width = min(256, chunk_bins)
    steps = chunk_bins // width
    shift = chunk * steps
    whole = lambda: pl.BlockSpec(
        fwd.shape, lambda step: (0, 0, 0), pipeline_mode=pl.Buffered(1)
    )
    return pl.pallas_call(
        azimuth_kernel,
        grid=(steps,),
        in_specs=[
            pl.BlockSpec((outer_count, 2, rows, width), lambda step: (0, 0, 0, step)),
            pl.BlockSpec((2, TAPS, width), lambda step: (0, 0, step + shift)),
            pl.BlockSpec((1, width), lambda step: (0, step + shift)),
            whole(),
            whole(),
        ],
        out_specs=pl.BlockSpec((2, PULSES, width), lambda step: (0, 0, step)),
        out_shape=jax.ShapeDtypeStruct((2, PULSES, chunk_bins), jnp.bfloat16),
        compiler_params=pltpu.CompilerParams(vmem_limit_bytes=58 * 1024 * 1024),
        cost_estimate=pl.CostEstimate(
            flops=steps * 4 * 2 * 1024 * 1024 * 3 * width,
            bytes_accessed=columns.size * 5 + 2 * fwd.size * 2,
            transcendentals=0,
        ),
    )(columns, replicas, lengths, fwd, inv)


def body(echoes, chirp_taps, replicas, lengths):
    sub_count = lax.axis_size("sub")
    outer_count = lax.axis_size(("az", "sec"))
    own_bins = replicas.shape[2]
    halo = lax.ppermute(
        echoes[:, :, :CHIRP],
        "sub",
        [(i, (i - 1) % sub_count) for i in range(sub_count)],
    )
    chunks = max(1, min(CHUNKS, own_bins // 128))
    width = min(256, own_bins // chunks)
    cosine = toeplitz(chirp_taps[0].astype(jnp.bfloat16), width)
    sine = toeplitz(chirp_taps[1].astype(jnp.bfloat16), width)
    real_table = jnp.concatenate([cosine, -sine], axis=1)
    imag_table = jnp.concatenate([sine, cosine], axis=1)
    fwd = jnp.asarray(azimuth_tables())
    inv = jnp.swapaxes(fwd, 1, 2)
    extended = jnp.concatenate([echoes, halo], axis=2)
    counts = lengths[None, :]
    crossed = []
    for chunk in range(chunks):
        pieces = compress(
            extended, real_table, imag_table, chunk, chunks, sub_count, outer_count, own_bins
        )
        crossed.append(lax.all_to_all(pieces, "sub", split_axis=0, concat_axis=0, tiled=True))
    results = []
    for chunk in range(chunks):
        pieces = crossed[chunk].reshape((outer_count,) + crossed[chunk].shape[2:])
        columns = lax.all_to_all(pieces, ("az", "sec"), split_axis=0, concat_axis=0, tiled=True)
        results.append(focus(columns, replicas, counts, fwd, inv, chunk))
    return jnp.concatenate(results, axis=2)


def solution(mesh):
    placed = (
        P(None, ("grp", "az", "sec"), "sub"),
        P(),
        P(None, None, ("grp", "az", "sec", "sub")),
        P(("grp", "az", "sec", "sub")),
    )
    return jax.shard_map(
        body,
        mesh=mesh,
        in_specs=placed,
        out_specs=P(None, None, ("grp", "az", "sec", "sub")),
        check_vma=False,
    )
```

```python
import functools
import math

import jax
import jax.numpy as jnp
import numpy as np
from jax import lax
from jax.experimental import pallas as pl
from jax.experimental.pallas import tpu as pltpu
from jax.sharding import PartitionSpec as P

CHIRP = 2048
TAPS = 1024
PULSES = 2048
QUARTER = PULSES // 4
CHUNKS = 4


def azimuth_tables():
    j = np.arange(QUARTER)[:, None]
    b = np.arange(QUARTER)[None, :]
    tables = []
    for t in range(4):
        angles = -2.0 * math.pi / PULSES * ((b * (4 * j + t)) % PULSES)
        cosine, sine = np.cos(angles), np.sin(angles)
        tables.append(np.block([[cosine, -sine], [sine, cosine]]))
    return np.stack(tables).astype(np.float32).astype(jnp.bfloat16)


def toeplitz(taps, width):
    depth = CHIRP + width
    length = depth + width
    padded = jnp.pad(taps, (0, length - CHIRP))
    flat = jnp.tile(padded, width)[: width * (length - 1)]
    return flat.reshape(width, length - 1)[:, :depth].T


def range_kernel(width, order, echo_ref, real_ref, imag_ref, out_ref):
    start = pl.multiple_of(order(pl.program_id(0)) * width, width)
    depth = CHIRP + width
    both = jnp.dot(
        echo_ref[0, :, pl.ds(start, depth)], real_ref[...], preferred_element_type=jnp.float32
    ) + jnp.dot(
        echo_ref[1, :, pl.ds(start, depth)], imag_ref[...], preferred_element_type=jnp.float32
    )
    out_ref[0, 0, 0] = both[:, :width].astype(jnp.bfloat16)
    out_ref[0, 0, 1] = both[:, width:].astype(jnp.bfloat16)


def compress(
    extended, real_table, imag_table, chunk, chunks, sub_count, outer_count, own_bins
):
    rows = extended.shape[1]
    width = real_table.shape[1] // 2
    chunk_bins = own_bins // chunks
    per_chunk = chunk_bins // width
    per_dest = own_bins // width

    def order(step):
        return (step // per_chunk) * per_dest + chunk * per_chunk + step % per_chunk

    def place(step):
        dest = step // per_chunk
        return (dest % sub_count, dest // sub_count, 0, 0, step % per_chunk)

    whole = lambda *shape: pl.BlockSpec(
        shape, lambda step: (0,) * len(shape), pipeline_mode=pl.Buffered(1)
    )
    steps = outer_count * per_chunk
    return pl.pallas_call(
        functools.partial(range_kernel, width, order),
        grid=(steps,),
        in_specs=[
            whole(*extended.shape),
            whole(*real_table.shape),
            whole(*imag_table.shape),
        ],
        out_specs=pl.BlockSpec((1, 1, 2, rows, width), place),
        out_shape=jax.ShapeDtypeStruct(
            (sub_count, outer_count // sub_count, 2, rows, chunk_bins), jnp.bfloat16
        ),
        compiler_params=pltpu.CompilerParams(vmem_limit_bytes=48 * 1024 * 1024),
        cost_estimate=pl.CostEstimate(
            flops=steps * 4 * rows * real_table.shape[0] * 2 * width,
            bytes_accessed=2 * extended.size + 2 * steps * 2 * rows * width,
            transcendentals=0,
        ),
    )(extended, real_table, imag_table)


def turn(pair, count):
    real, imag = pair
    return ((real, imag), (-imag, real), (-real, -imag), (imag, -real))[count % 4]


def combine(pairs, direction, t):
    turned = [turn(pair, direction * a * t) for a, pair in enumerate(pairs)]
    real, imag = turned[0]
    for other_real, other_imag in turned[1:]:
        real, imag = real + other_real, imag + other_imag
    return real, imag


def azimuth_kernel(column_ref, replica_ref, count_ref, fwd_ref, inv_ref, out_ref):
    bins = out_ref.shape[-1]
    f32 = jnp.float32
    column = [column_ref[:, s].reshape(4, QUARTER, bins) for s in range(2)]
    column = [(column[0][a].astype(f32), column[1][a].astype(f32)) for a in range(4)]
    position = lax.broadcasted_iota(jnp.int32, (TAPS, bins), 0)
    kept = position < count_ref[...]
    taps = [jnp.where(kept, replica_ref[s].astype(f32), 0.0) for s in range(2)]
    taps = [
        (taps[0][a * QUARTER : (a + 1) * QUARTER], taps[1][a * QUARTER : (a + 1) * QUARTER])
        for a in range(TAPS // QUARTER)
    ]
    parts = []
    for t in range(4):
        sides = []
        for pieces in (column, taps):
            mixed = jnp.concatenate(combine(pieces, -1, t), axis=0).astype(jnp.bfloat16)
            found = jnp.dot(fwd_ref[t], mixed, preferred_element_type=f32)
            sides.append((found[:QUARTER], found[QUARTER:]))
        (x_real, x_imag), (q_real, q_imag) = sides
        y_real = (x_real * q_real + x_imag * q_imag) * (1.0 / PULSES)
        y_imag = (x_imag * q_real - x_real * q_imag) * (1.0 / PULSES)
        y = jnp.concatenate([y_real, y_imag], axis=0).astype(jnp.bfloat16)
        back = jnp.dot(inv_ref[t], y, preferred_element_type=f32)
        parts.append((back[:QUARTER], back[QUARTER:]))
    for a in range(4):
        real, imag = combine(parts, 1, a)
        out_ref[0, a * QUARTER : (a + 1) * QUARTER] = real.astype(jnp.bfloat16)
        out_ref[1, a * QUARTER : (a + 1) * QUARTER] = imag.astype(jnp.bfloat16)


def focus(columns, replicas, lengths, fwd, inv, chunk):
    outer_count, _, rows, chunk_bins = columns.shape
    width = min(256, chunk_bins)
    steps = chunk_bins // width
    shift = chunk * steps
    whole = lambda: pl.BlockSpec(
        fwd.shape, lambda step: (0, 0, 0), pipeline_mode=pl.Buffered(1)
    )
    return pl.pallas_call(
        azimuth_kernel,
        grid=(steps,),
        in_specs=[
            pl.BlockSpec((outer_count, 2, rows, width), lambda step: (0, 0, 0, step)),
            pl.BlockSpec((2, TAPS, width), lambda step: (0, 0, step + shift)),
            pl.BlockSpec((1, width), lambda step: (0, step + shift)),
            whole(),
            whole(),
        ],
        out_specs=pl.BlockSpec((2, PULSES, width), lambda step: (0, 0, step)),
        out_shape=jax.ShapeDtypeStruct((2, PULSES, chunk_bins), jnp.bfloat16),
        compiler_params=pltpu.CompilerParams(vmem_limit_bytes=58 * 1024 * 1024),
        cost_estimate=pl.CostEstimate(
            flops=steps * 4 * 2 * 1024 * 1024 * 3 * width,
            bytes_accessed=columns.size * 5 + 2 * fwd.size * 2,
            transcendentals=0,
        ),
    )(columns, replicas, lengths, fwd, inv)


def exchange(pieces, sub_count):
    me = lax.axis_index("sub")
    result = pieces
    for step in range(1, sub_count):
        target = lax.rem(me + step, sub_count)
        source = lax.rem(me + sub_count - step, sub_count)
        moved = lax.ppermute(
            lax.dynamic_index_in_dim(pieces, target, 0),
            "sub",
            [(i, (i + step) % sub_count) for i in range(sub_count)],
        )
        result = lax.dynamic_update_slice_in_dim(result, moved, source, 0)
    return result


def body(echoes, chirp_taps, replicas, lengths):
    sub_count = lax.axis_size("sub")
    outer_count = lax.axis_size(("az", "sec"))
    own_bins = replicas.shape[2]
    halo = lax.ppermute(
        echoes[:, :, :CHIRP],
        "sub",
        [(i, (i - 1) % sub_count) for i in range(sub_count)],
    )
    chunks = max(1, min(CHUNKS, own_bins // 128))
    width = min(256, own_bins // chunks)
    cosine = toeplitz(chirp_taps[0].astype(jnp.bfloat16), width)
    sine = toeplitz(chirp_taps[1].astype(jnp.bfloat16), width)
    real_table = jnp.concatenate([cosine, -sine], axis=1)
    imag_table = jnp.concatenate([sine, cosine], axis=1)
    fwd = jnp.asarray(azimuth_tables())
    inv = jnp.swapaxes(fwd, 1, 2)
    extended = jnp.concatenate([echoes, halo], axis=2)
    counts = lengths[None, :]
    crossed = []
    for chunk in range(chunks):
        pieces = compress(
            extended, real_table, imag_table, chunk, chunks, sub_count, outer_count, own_bins
        )
        crossed.append(exchange(pieces, sub_count))
    results = []
    for chunk in range(chunks):
        pieces = crossed[chunk].reshape((outer_count,) + crossed[chunk].shape[2:])
        columns = lax.all_to_all(pieces, ("az", "sec"), split_axis=0, concat_axis=0, tiled=True)
        results.append(focus(columns, replicas, counts, fwd, inv, chunk))
    return jnp.concatenate(results, axis=2)


def solution(mesh):
    placed = (
        P(None, ("grp", "az", "sec"), "sub"),
        P(),
        P(None, None, ("grp", "az", "sec", "sub")),
        P(("grp", "az", "sec", "sub")),
    )
    return jax.shard_map(
        body,
        mesh=mesh,
        in_specs=placed,
        out_specs=P(None, None, ("grp", "az", "sec", "sub")),
        check_vma=False,
    )
```
